128 devices in a mesh: views: 4 (over z_hi, core), slab: 32 (over z_lo, y, x).
Axes of the slice: x: 4, y: 4, z: 4 (z_hi: 2, z_lo: 2; z = z_hi * 2 + z_lo), core: 2. Of those that a mesh axis runs over, the one named last changes fastest.
Arguments:
- tiles: bfloat16 [2, 32, 640, 16, 256], P(None, 'slab', 'views'), may hold values from 0 to 0.25
- lor_weight: bfloat16 [2, 32, 640, 16], P(None, 'slab', 'views'), may hold values from 0.049804688 to 1
- block_map: int32 [2, 32, 640], P(None, 'slab', 'views'), may hold values from 0 to 2699
- kernel_weight: bfloat16 [147, 32, 230400], P(None, 'slab', 'views'), may hold values from 0 to 0.04, as said below
Outputs:
- sensitivity: float32 [32, 230400], P('slab', 'views')
The draws below stay inside these ranges and needn't reach their ends.
Inputs may be any that keep to these rules, and one draw needn't show every extreme that they name: `kernel_weight`: for each voxel exactly 50 of its 147 box entries are nonzero (its kernel neighbours); the others are zero.
All inputs are finite; a program needn't handle non-finite values.
Results may differ from the reference program's by a relative error of at most 0.0003.
Values sent between devices are 32-bit elements; how exact they have to be, the bound alone decides.
A program may use at most 384 MiB of HBM per device.

```python
import math
import jax
import jax.numpy as jnp
import numpy as np
from jax import lax

SUB = 2
LT = 16
VB = 256
PZ = 1
NCOL = 480
KN = 50
BOX = 147
SLABS = 32
NZ = 32
NROW = 480
NXY = 230400
TV = 640
EXT_BLK = 2700


def draw_kernel_weight(key, part):
    key = jax.random.fold_in(key, 11)
    first, second, third = jax.random.split(key, 3)
    stride_table = jnp.array(np.array([v for v in range(1, 147) if v % 3 != 0 and v % 7 != 0], dtype=np.int32))
    begin_box = jax.random.randint(first, (1, NZ, NXY), 0, 147)
    stride_index = jax.random.randint(second, (1, NZ, NXY), 0, stride_table.shape[0])
    stride_value = stride_table[stride_index]
    entry = jnp.arange(BOX, dtype=jnp.int32)[:, None, None]
    ranked = (entry * stride_value + begin_box) % 147
    chosen = ranked < KN
    spread = jax.random.uniform(third, (BOX, NZ, NXY), jnp.float32, jnp.log(0.002), jnp.log(0.039))
    values = jnp.exp(spread)
    return jnp.where(chosen, values, 0.0).astype(jnp.bfloat16)


def place_ends(values, key, least, high):
    index_at = [jax.random.randint(jax.random.fold_in(key, axis), (), 0, length) for axis, length in enumerate(values.shape)]
    longest = values.shape.index(max(values.shape))
    beside = index_at[:longest] + [(index_at[longest] + 1) % values.shape[longest]] + index_at[longest + 1:]
    return values.at[tuple(index_at)].set(least).at[tuple(beside)].set(high)


def block_scale(rng, extent, cuts, smallest, top_value):
    gain = 1.0
    for position, blocks in cuts:
        draws = jax.random.uniform(jax.random.fold_in(jax.random.fold_in(rng, 6), position), (blocks,), jnp.float32, smallest / len(cuts), top_value / len(cuts))
        gain = gain * jnp.repeat(jnp.exp(draws), extent[position] // blocks).reshape((-1,) + (1,) * (len(extent) - 1 - position))
    return gain


def setup_inputs(seed: int = 0) -> dict:
    arg_keys = jax.random.split(jax.random.key(seed), 5)
    return {
        "tiles": jnp.clip(0.25 * jax.random.uniform(arg_keys[0], (SUB, SLABS, TV, LT, VB), jnp.float32) ** block_scale(arg_keys[0], (SUB, SLABS, TV, LT, VB), ((1, 32), (2, 4)), -0.2, 0.2), 0.0, 0.25).astype(jnp.bfloat16),
        "lor_weight": jnp.clip(jnp.exp(math.log(1.0) - 2.9996462 * jax.random.uniform(arg_keys[1], (SUB, SLABS, TV, LT), jnp.float32) ** block_scale(arg_keys[1], (SUB, SLABS, TV, LT), ((1, 32), (2, 4)), -0.2, 0.2)), 0.049804688, 1.0).astype(jnp.bfloat16),
        "block_map": place_ends(jax.random.randint(arg_keys[2], (SUB, SLABS, TV), 0, EXT_BLK), jax.random.fold_in(arg_keys[2], 1), 0, EXT_BLK - 1).astype(jnp.int32),
        "kernel_weight": draw_kernel_weight(jax.random.fold_in(arg_keys[4], 71), 0),
    }


def reference(tiles, lor_weight, block_map, kernel_weight):
    nplanes = PZ * SLABS
    wide = NXY
    padded = jnp.zeros((nplanes + 2 * PZ, wide), jnp.float32)

    def add_slab(carry, index):
        tile_part = lax.dynamic_index_in_dim(tiles, index, 1, False).astype(jnp.float32)
        weight_part = lax.dynamic_index_in_dim(lor_weight, index, 1, False).astype(jnp.float32)
        map_part = lax.dynamic_index_in_dim(block_map, index, 1, False)
        contrib = jnp.einsum("atlv,atl->atv", tile_part, weight_part)
        extended = jax.ops.segment_sum(contrib.reshape(-1, VB), map_part.reshape(-1), num_segments=EXT_BLK)
        extended = extended.reshape(3 * PZ, wide)
        start = (index * PZ).astype(jnp.int32)
        zero = jnp.zeros((), jnp.int32)
        current = lax.dynamic_slice(carry, (start, zero), (3 * PZ, wide))
        return lax.dynamic_update_slice(carry, current + extended, (start, zero)), None

    padded, _ = lax.scan(add_slab, padded, jnp.arange(SLABS, dtype=jnp.int32))
    image = padded[PZ:PZ + nplanes].reshape(nplanes, NROW, NCOL)
    framed = jnp.pad(image, ((1, 1), (3, 3), (3, 3)))
    total = jnp.zeros((nplanes, NROW, NCOL), jnp.float32)
    for entry in range(BOX):
        plane_start = entry // 49
        row_start = (entry // 7) % 7
        column_start = entry % 7
        moved = framed[plane_start:plane_start + nplanes, row_start:row_start + NROW, column_start:column_start + NCOL]
        weight = kernel_weight[entry].astype(jnp.float32).reshape(nplanes, NROW, NCOL)
        total = total + weight * moved
    return total.reshape(nplanes, wide)
```

```python
import functools

import jax
import jax.numpy as jnp
from jax import lax
from jax.experimental import pallas as pl
from jax.experimental.pallas import tpu as pltpu
from jax.sharding import PartitionSpec as P

MESH = pl.DeviceIdType.MESH
NCOL = 480
LANES = 128
BLOCK = 256
HALO = 6
BANDED = 240
ROWS = 2 * BANDED
LEAD = 2 * HALO
CHUNKS = 4
CHUNK = ROWS // CHUNKS
PIECES = 4
TOP = 8
STRIP = 16
RING = 4
PHASE = [(NCOL * dy) % LANES // 32 for dy in range(-3, 4)]
WHOLE = [LEAD + (NCOL * dy) // LANES for dy in range(-3, 4)]


def kernel(
    plane_blocks, tiles_hbm, lor_ref, map_ref, kw_hbm, out_ref,
    tiles, raw, raw_tail, stage, weights, contrib, keys, band, zsend, zrecv, plane, column, shifted, partial,
    tile_sem, raw_sem, tail_sem, raw_send, raw_recv, sib_send, sib_recv, fwd_send, fwd_recv, key_send, key_recv,
    z_send, z_recv, x_send, x_recv,
):
    subsets, lors, per_dev = lor_ref.shape
    entries, voxels = kw_hbm.shape
    count = subsets * per_dev
    piece = count // PIECES
    band_blocks = voxels // BLOCK
    out_rows = voxels // LANES
    full = out_rows // STRIP
    tail_rows = out_rows - full * STRIP
    strip_lanes = STRIP * LANES

    v = lax.axis_index("views")
    s = lax.axis_index("slab")
    slabs = lax.axis_size("slab")
    sibling = (v // 2 * 2 + 1 - lax.rem(v, 2), s)
    opposite = lax.rem(v + 2, 4)
    across = (opposite, s)
    above = (v, lax.rem(s + 1, slabs))
    below = (v, lax.rem(s + slabs - 1, slabs))

    barrier = pltpu.get_barrier_semaphore()
    for device in (sibling, across, above, below):
        pl.semaphore_signal(barrier, inc=1, device_id=device, device_id_type=MESH)

    def remote(src, dst, send, recv, device):
        return pltpu.make_async_remote_copy(
            src_ref=src, dst_ref=dst, send_sem=send, recv_sem=recv, device_id=device, device_id_type=MESH
        )

    tile_rows = per_dev * lors
    tile_loads = [
        pltpu.make_async_copy(
            tiles_hbm.at[pl.ds(u * tile_rows, tile_rows)], tiles.at[pl.ds(u * tile_rows, tile_rows)], tile_sem.at[u]
        )
        for u in range(subsets)
    ]
    for load in tile_loads:
        load.start()

    def raw_load(t, slot):
        start = t * strip_lanes if isinstance(t, int) else pl.multiple_of(t * strip_lanes, strip_lanes)
        return pltpu.make_async_copy(kw_hbm.at[:, pl.ds(start, strip_lanes)], raw.at[slot], raw_sem.at[slot])

    tail_load = pltpu.make_async_copy(
        kw_hbm.at[:, pl.ds(full * strip_lanes, tail_rows * LANES)], raw_tail, tail_sem.at[0]
    )
    for t in range(RING):
        raw_load(t, t).start()
    tail_load.start()

    width = keys.shape[2]
    pad = jnp.full((1, width - count), -1, jnp.int32)
    row = jnp.concatenate([map_ref[u] for u in range(subsets)] + [pad], axis=1)
    keys[0] = jnp.broadcast_to(row, keys.shape[1:])
    spread = (
        lax.rem(lax.broadcasted_iota(jnp.int32, (lors, BLOCK), 1), lors)
        == lax.broadcasted_iota(jnp.int32, (lors, BLOCK), 0)
    ).astype(jnp.float32).astype(jnp.bfloat16)
    group = BLOCK // lors
    diagonal = (
        lax.rem(lax.broadcasted_iota(jnp.int32, (per_dev, BLOCK), 0), group)
        == lax.broadcasted_iota(jnp.int32, (per_dev, BLOCK), 1) // lors
    )
    for u in range(subsets):
        wide = lax.dot_general(
            lor_ref[u], spread, (((0,), (0,)), ((), ())), preferred_element_type=jnp.float32
        )
        wide = jnp.where(diagonal, wide, 0.0).astype(jnp.bfloat16)
        tile_loads[u].wait()
        for k in range(per_dev // group):
            first = (u * per_dev + k * group) * lors
            contrib[0, pl.ds(u * per_dev + k * group, group), :] = jnp.dot(
                wide[k * group : (k + 1) * group], tiles[pl.ds(first, BLOCK), :], preferred_element_type=jnp.float32
            )

    pl.semaphore_wait(barrier, 4)

    to_x, to_fwd, key_copies = [], [], []
    for n in range(PIECES):
        rows = pl.ds(n * piece, piece)
        pair = []
        for side, (target, device) in enumerate(((1, above), (2, below))):
            pair.append(
                remote(contrib.at[0, rows], contrib.at[target, rows], raw_send.at[side, n], raw_recv.at[side, n], device)
            )
        to_x.append(pair)
        to_fwd.append(
            [
                remote(
                    contrib.at[side + 1, rows], contrib.at[side + 4, rows],
                    fwd_send.at[side, n], fwd_recv.at[side, n], sibling,
                )
                for side in range(2)
            ]
        )
    for n, (source, target, device) in enumerate(
        ((0, 1, above), (0, 2, below), (0, 3, sibling), (1, 4, sibling), (2, 5, sibling))
    ):
        key_copies.append(remote(keys.at[source], keys.at[target], key_send.at[n], key_recv.at[n], device))
    for n in range(3):
        key_copies[n].start()
    for pair in to_x:
        for copy in pair:
            copy.start()
    to_sibling = remote(contrib.at[0], contrib.at[3], sib_send.at[0], sib_recv.at[0], sibling)
    to_sibling.start()

    shape = column.shape
    column[...] = lax.rem(
        LANES * lax.broadcasted_iota(jnp.int32, shape, 0)
        + lax.broadcasted_iota(jnp.int32, shape, 1)
        + (10 * NCOL - (TOP + LEAD) * LANES),
        NCOL,
    )

    def turn(source, rows, start):
        for base in range(0, entries, 16):
            size = min(16, entries - base)
            for c in range(rows):
                stage[pl.ds(base * STRIP + c * 16, size), :] = source[
                    pl.ds(base, size), pl.ds(c * LANES, LANES)
                ].astype(jnp.float32)
            for e in range(size):
                weights[base + e, pl.ds(start, STRIP), :] = stage[
                    pl.ds(base * STRIP + e, STRIP, stride=16), :
                ].astype(jnp.bfloat16)

    def turn_strips(low, high):
        @pl.loop(low, high)
        def _(t):
            slot = lax.rem(t, RING)
            raw_load(t, slot).wait()
            turn(raw.at[slot], STRIP, pl.multiple_of(t * STRIP, STRIP))

            @pl.when(t + RING < full)
            def _():
                raw_load(t + RING, slot).start()

    def scatter(sets, into, first):
        for index in sets:
            delta = (0, -1, 1)[index % 3]
            whole = contrib[index]
            high = whole.astype(jnp.bfloat16)
            low = (whole - high.astype(jnp.float32)).astype(jnp.bfloat16)
            place = keys[index][0:1, 0:count] - plane_blocks * (1 - delta)
            if delta < 0:
                place = jnp.where(s > 0, place, -1)
            if delta > 0:
                place = jnp.where(s < slabs - 1, place, -1)
            inside = (place >= 0) & (place < plane_blocks)
            for n, view in enumerate((opposite, v)):
                target = jnp.where(inside, place - (band_blocks * view - HALO), -1)
                chosen = lax.broadcasted_iota(jnp.int32, (BANDED, count), 0) == target
                chosen = jnp.where(chosen, 1.0, 0.0).astype(jnp.bfloat16)
                total = jnp.dot(chosen, high, preferred_element_type=jnp.float32) + jnp.dot(
                    chosen, low, preferred_element_type=jnp.float32
                )
                if first and index == sets[0]:
                    into[n] = total
                else:
                    into[n] = into[n] + total

    marks = [full * n // PIECES for n in range(PIECES + 1)]
    for n in range(PIECES):
        turn_strips(marks[n], marks[n + 1])
        if n == 0:
            key_copies[2].wait_recv()
            to_sibling.wait_recv()
            scatter((0, 3), band, True)
            for k in range(2):
                key_copies[k].wait_recv()
                key_copies[3 + k].start()
        for side in range(2):
            to_x[n][side].wait_recv()
            to_fwd[n][side].start()
    tail_load.wait()
    turn(raw_tail, tail_rows, full * STRIP)
    scatter((1, 2), band, False)
    for n in range(PIECES):
        for side in range(2):
            to_fwd[n][side].wait_recv()
    for k in range(2):
        key_copies[3 + k].wait_recv()
    scatter((4, 5), band, False)

    for half in range(2):
        lanes = pl.ds(half * LANES, LANES)
        zsend[pl.ds(half, BANDED, stride=2), :] = band[0, :, lanes]
    to_across = []
    for c in range(CHUNKS):
        rows = pl.ds(c * CHUNK, CHUNK)
        to_across.append(remote(zsend.at[rows], zrecv.at[rows], z_send.at[c], z_recv.at[c], across))
        to_across[c].start()
    for half in range(2):
        lanes = pl.ds(half * LANES, LANES)
        plane[1, pl.ds(TOP + half, BANDED, stride=2), :] = band[1, :, lanes]

    lane = lax.broadcasted_iota(jnp.int32, (8, LANES), 1)

    def shift(d, keep, low, high):
        @pl.loop(low, high)
        def _(t):
            k = pl.multiple_of(t * 8, 8)
            near = []
            for offset in (-1, 0, 1):
                values = plane[d, pl.ds(TOP + offset + k, 8), :]
                near.append(
                    (values if keep is None else values * keep, column[pl.ds(TOP + offset + k, 8), :])
                )
            for dx in range(-3, 4):

                def masked(n):
                    values, col = near[n]
                    if dx == 0:
                        return values
                    return jnp.where(col >= dx if dx > 0 else col < NCOL + dx, values, 0.0)

                here, after = masked(1), masked(2)
                for phase in range(4):
                    a = 32 * phase + dx
                    if a == 0:
                        moved = here
                    elif a > 0:
                        moved = pltpu.roll(jnp.where(lane >= a, here, after), LANES - a, 1)
                    else:
                        moved = pltpu.roll(jnp.where(lane < LANES + a, here, masked(0)), -a, 1)
                    shifted[d * 28 + phase * 7 + dx + 3, pl.ds(k, 8), :] = moved

    def box(planes, start):
        sums = [None] * 4
        for d in planes:
            for dy in range(7):
                for dx in range(7):
                    weight = weights[d * 49 + dy * 7 + dx, pl.ds(start, STRIP), :].astype(jnp.float32)
                    term = weight * shifted[d * 28 + PHASE[dy] * 7 + dx, pl.ds(start + WHOLE[dy], STRIP), :]
                    n = dx % 4
                    sums[n] = term if sums[n] is None else sums[n] + term
        return (sums[0] + sums[1]) + (sums[2] + sums[3])

    def box_own(low, high):
        @pl.loop(low, high)
        def _(t):
            start = pl.multiple_of(t * STRIP, STRIP)
            partial[pl.ds(start, STRIP), :] = box((1,), start)

    def box_sides(low, high):
        @pl.loop(low, min(high, full))
        def _(t):
            start = pl.multiple_of(t * STRIP, STRIP)
            out_ref[pl.ds(start, STRIP), :] = box((0, 2), start) + partial[pl.ds(start, STRIP), :]

        if high > full:
            start = full * STRIP
            total = box((0, 2), start) + partial[pl.ds(start, STRIP), :]
            out_ref[pl.ds(start, tail_rows), :] = total[0:tail_rows]

    shift_marks = [0] + [CHUNK * (c + 1) // 8 - 1 for c in range(CHUNKS - 1)] + [ROWS // 8]
    box_marks = [0] + [(8 * m - (STRIP - 1 + max(WHOLE)) - 1) // STRIP + 1 for m in shift_marks[1:-1]] + [full + 1]

    to_sides = []
    for c in range(CHUNKS):
        rows = pl.ds(c * CHUNK, CHUNK)
        inner = pl.ds(TOP + c * CHUNK, CHUNK)
        to_across[c].wait_recv()
        plane[1, inner, :] = plane[1, inner, :] + zrecv[rows, :]
        to_sides.append(
            [
                remote(plane.at[1, inner], plane.at[target, inner], x_send.at[side, c], x_recv.at[side, c], device)
                for side, (target, device) in enumerate(((0, above), (2, below)))
            ]
        )
        for copy in to_sides[c]:
            copy.start()
        shift(1, None, shift_marks[c], shift_marks[c + 1])
        box_own(box_marks[c], box_marks[c + 1])
    low_keep = (s > 0).astype(jnp.float32)
    high_keep = (s < slabs - 1).astype(jnp.float32)
    for c in range(CHUNKS):
        for copy in to_sides[c]:
            copy.wait_recv()
        shift(0, low_keep, shift_marks[c], shift_marks[c + 1])
        shift(2, high_keep, shift_marks[c], shift_marks[c + 1])
        box_sides(box_marks[c], box_marks[c + 1])

    for copies in to_x + to_fwd + to_sides + [to_across, key_copies, [to_sibling]]:
        for copy in copies:
            copy.wait_send()


def per_device(tiles, lor_weight, block_map, kernel_weight):
    subsets, _, per_dev, lors, width = tiles.shape
    entries, planes, voxels = kernel_weight.shape
    plane_blocks = voxels * lax.axis_size("views") // width
    count = subsets * per_dev
    out_rows = voxels // LANES
    strips = -(-out_rows // STRIP)
    tail = out_rows - (strips - 1) * STRIP
    hbm = pl.BlockSpec(memory_space=pl.ANY)
    vmem = pl.BlockSpec(memory_space=pltpu.VMEM)
    dma = pltpu.SemaphoreType.DMA
    out = pl.pallas_call(
        functools.partial(kernel, plane_blocks),
        out_shape=jax.ShapeDtypeStruct((out_rows, LANES), jnp.float32),
        in_specs=[hbm, vmem, vmem, hbm],
        out_specs=vmem,
        scratch_shapes=[
            pltpu.VMEM((count * lors, width), jnp.bfloat16),
            pltpu.VMEM((RING, entries, STRIP * LANES), jnp.bfloat16),
            pltpu.VMEM((entries, tail * LANES), jnp.bfloat16),
            pltpu.VMEM((160 * STRIP, LANES), jnp.float32),
            pltpu.VMEM((entries, strips * STRIP, LANES), jnp.bfloat16),
            pltpu.VMEM((6, count, width), jnp.float32),
            pltpu.VMEM((6, 8, 384), jnp.int32),
            pltpu.VMEM((2, BANDED, width), jnp.float32),
            pltpu.VMEM((ROWS, LANES), jnp.float32),
            pltpu.VMEM((ROWS, LANES), jnp.float32),
            pltpu.VMEM((3, ROWS + 2 * TOP, LANES), jnp.float32),
            pltpu.VMEM((ROWS + 2 * TOP, LANES), jnp.int32),
            pltpu.VMEM((84, ROWS + TOP, LANES), jnp.float32),
            pltpu.VMEM((strips * STRIP, LANES), jnp.float32),
            dma((subsets,)),
            dma((RING,)),
            dma((1,)),
            dma((2, PIECES)),
            dma((2, PIECES)),
            dma((1,)),
            dma((1,)),
            dma((2, PIECES)),
            dma((2, PIECES)),
            dma((5,)),
            dma((5,)),
            dma((CHUNKS,)),
            dma((CHUNKS,)),
            dma((2, CHUNKS)),
            dma((2, CHUNKS)),
        ],
        compiler_params=pltpu.CompilerParams(
            collective_id=0, has_side_effects=True, vmem_limit_bytes=60 * 1024 * 1024
        ),
    )(
        tiles.reshape(count * lors, width),
        jnp.transpose(lor_weight.reshape(subsets, per_dev, lors), (0, 2, 1)),
        block_map.reshape(subsets, 1, per_dev),
        kernel_weight.reshape(entries, voxels),
    )
    return out.reshape(planes, voxels)


def solution(mesh):
    placed = (
        P(None, "slab", "views", None, None),
        P(None, "slab", "views", None),
        P(None, "slab", "views"),
        P(None, "slab", "views"),
    )
    return jax.shard_map(
        per_device, mesh=mesh, in_specs=placed, out_specs=P("slab", "views"), check_vma=False
    )
```

```python
import functools

import jax
import jax.numpy as jnp
from jax import lax
from jax.experimental import pallas as pl
from jax.experimental.pallas import tpu as pltpu
from jax.sharding import PartitionSpec as P

MESH = pl.DeviceIdType.MESH
NCOL = 480
LANES = 128
BLOCK = 256
HALO = 6
BANDED = 240
ROWS = 2 * BANDED
LEAD = HALO * BLOCK - 3 * NCOL
QUAD = 4 * NCOL // LANES
PARTS = 4
MARKS = (0, 128, 248, 368, ROWS)
CHUNKS = len(MARKS) - 1
BOX_MARKS = (0, 3, 7, 11, 15)
PIECES = 4
AHEAD = 2
RING = 8


def kernel(
    plane_blocks, tiles_hbm, lor_ref, map_ref, kw_hbm, out_ref,
    tiles, raw, weights, contrib, keys, band, zsend, zrecv, plane, shifted, result,
    tile_sem, raw_sem, raw_send, raw_recv, sib_send, sib_recv, fwd_send, fwd_recv, key_send, key_recv,
    z_send, z_recv, x_send, x_recv,
):
    subsets, lors, per_dev = lor_ref.shape
    entries, voxels = kw_hbm.shape
    count = subsets * per_dev
    piece = count // PIECES
    band_blocks = voxels // BLOCK
    quads = voxels // (QUAD * LANES)

    v = lax.axis_index("views")
    s = lax.axis_index("slab")
    slabs = lax.axis_size("slab")
    sibling = (v // 2 * 2 + 1 - lax.rem(v, 2), s)
    opposite = lax.rem(v + 2, 4)
    across = (opposite, s)
    above = (v, lax.rem(s + 1, slabs))
    below = (v, lax.rem(s + slabs - 1, slabs))

    barrier = pltpu.get_barrier_semaphore()
    for device in (sibling, across, above, below):
        pl.semaphore_signal(barrier, inc=1, device_id=device, device_id_type=MESH)

    def remote(src, dst, send, recv, device):
        return pltpu.make_async_remote_copy(
            src_ref=src, dst_ref=dst, send_sem=send, recv_sem=recv, device_id=device, device_id_type=MESH
        )

    piece_rows = piece * lors
    tile_loads = [
        pltpu.make_async_copy(
            tiles_hbm.at[pl.ds(n * piece_rows, piece_rows)], tiles.at[pl.ds(n * piece_rows, piece_rows)], tile_sem.at[n]
        )
        for n in range(PIECES)
    ]
    for load in tile_loads:
        load.start()

    def raw_load(m, slot):
        lanes = QUAD * LANES
        start = m * lanes if isinstance(m, int) else pl.multiple_of(m * lanes, lanes)
        return pltpu.make_async_copy(kw_hbm.at[:, pl.ds(start, lanes)], raw.at[slot], raw_sem.at[slot])

    for m in range(RING):
        raw_load(m, m).start()

    to_x, to_fwd, key_copies = [], [], []
    for n in range(PIECES):
        rows = pl.ds(n * piece, piece)
        pair = []
        for side, (target, device) in enumerate(((1, above), (2, below))):
            pair.append(
                remote(contrib.at[0, rows], contrib.at[target, rows], raw_send.at[side, n], raw_recv.at[side, n], device)
            )
        to_x.append(pair)
        to_fwd.append(
            [
                remote(
                    contrib.at[side + 1, rows], contrib.at[side + 4, rows],
                    fwd_send.at[side, n], fwd_recv.at[side, n], sibling,
                )
                for side in range(2)
            ]
        )
    for n, (source, target, device) in enumerate(
        ((0, 1, above), (0, 2, below), (0, 3, sibling), (1, 4, sibling), (2, 5, sibling))
    ):
        key_copies.append(remote(keys.at[source], keys.at[target], key_send.at[n], key_recv.at[n], device))
    to_sibling = remote(contrib.at[0], contrib.at[3], sib_send.at[0], sib_recv.at[0], sibling)

    width = keys.shape[2]
    pad = jnp.full((1, width - count), -1, jnp.int32)
    row = jnp.concatenate([map_ref[u] for u in range(subsets)] + [pad], axis=1)
    keys[0] = jnp.broadcast_to(row, keys.shape[1:])
    spread = (
        lax.rem(lax.broadcasted_iota(jnp.int32, (lors, BLOCK), 1), lors)
        == lax.broadcasted_iota(jnp.int32, (lors, BLOCK), 0)
    ).astype(jnp.float32).astype(jnp.bfloat16)
    group = BLOCK // lors
    diagonal = (
        lax.rem(lax.broadcasted_iota(jnp.int32, (per_dev, BLOCK), 0), group)
        == lax.broadcasted_iota(jnp.int32, (per_dev, BLOCK), 1) // lors
    )
    wide = []
    for u in range(subsets):
        spread_out = lax.dot_general(
            lor_ref[u], spread, (((0,), (0,)), ((), ())), preferred_element_type=jnp.float32
        )
        wide.append(jnp.where(diagonal, spread_out, 0.0).astype(jnp.bfloat16))
    for n in range(PIECES):
        tile_loads[n].wait()
        for first in range(n * piece, (n + 1) * piece, group):
            own = first % per_dev
            contrib[0, pl.ds(first, group), :] = jnp.dot(
                wide[first // per_dev][own : own + group], tiles[pl.ds(first * lors, BLOCK), :],
                preferred_element_type=jnp.float32,
            )
        if n == 0:
            pl.semaphore_wait(barrier, 4)
            for k in range(3):
                key_copies[k].start()
        if n < AHEAD:
            for copy in to_x[n]:
                copy.start()
    to_sibling.start()

    lane16 = lax.broadcasted_iota(jnp.int32, (16, LANES), 1)

    def turn(slot, m):
        for base in range(0, entries, 16):
            size = min(16, entries - base)
            here = [raw[slot, pl.ds(base, size), pl.ds(c * LANES, LANES)] for c in range(QUAD)]
            for i in range(4):
                first, a = divmod(NCOL * i, LANES)
                for q in range(PARTS):
                    values = here[first + q]
                    if a:
                        if first + q + 1 < QUAD:
                            values = jnp.where(lane16[0:size] >= a, values, here[first + q + 1])
                        values = pltpu.roll(values, LANES - a, 1)
                    values = values.astype(jnp.float32)
                    for half in range(0, size, 8):
                        some = min(8, size - half)
                        weights[(base + half) // 8 * PARTS + q, pl.ds((4 * m + i) * 8, some), :] = values[
                            half : half + some
                        ]

    def turn_quads(low, high):
        @pl.loop(low, high)
        def _(m):
            slot = lax.rem(m, RING)
            raw_load(m, slot).wait()
            turn(slot, m)

            @pl.when(m + RING < quads)
            def _():
                raw_load(m + RING, slot).start()

    def scatter(sets, into, first):
        for index in sets:
            delta = (0, -1, 1)[index % 3]
            whole = contrib[index]
            high = whole.astype(jnp.bfloat16)
            low = (whole - high.astype(jnp.float32)).astype(jnp.bfloat16)
            place = keys[index][0:1, 0:count] - plane_blocks * (1 - delta)
            if delta < 0:
                place = jnp.where(s > 0, place, -1)
            if delta > 0:
                place = jnp.where(s < slabs - 1, place, -1)
            inside = (place >= 0) & (place < plane_blocks)
            for n, view in enumerate((opposite, v)):
                target = jnp.where(inside, place - (band_blocks * view - HALO), -1)
                chosen = lax.broadcasted_iota(jnp.int32, (BANDED, count), 0) == target
                chosen = jnp.where(chosen, 1.0, 0.0).astype(jnp.bfloat16)
                total = jnp.dot(chosen, high, preferred_element_type=jnp.float32) + jnp.dot(
                    chosen, low, preferred_element_type=jnp.float32
                )
                if first and index == sets[0]:
                    into[n] = total
                else:
                    into[n] = into[n] + total

    marks = [quads * n // (PIECES - AHEAD + 1) for n in range(PIECES - AHEAD + 2)]
    for n in range(PIECES - AHEAD + 1):
        turn_quads(marks[n], marks[n + 1])
        if n + AHEAD < PIECES:
            for copy in to_x[n + AHEAD]:
                copy.start()
    key_copies[2].wait_recv()
    to_sibling.wait_recv()
    scatter((0, 3), band, True)
    for k in range(2):
        key_copies[k].wait_recv()
        key_copies[3 + k].start()
    for n in range(PIECES):
        for side in range(2):
            to_x[n][side].wait_recv()
            to_fwd[n][side].start()
    scatter((1, 2), band, False)
    for k in range(2):
        key_copies[3 + k].wait_recv()
    for n in range(PIECES):
        for side in range(2):
            to_fwd[n][side].wait_recv()
    scatter((4, 5), band, False)

    for half in range(2):
        lanes = pl.ds(half * LANES, LANES)
        zsend[pl.ds(half, BANDED, stride=2), :] = band[0, :, lanes]
    chunk_rows = [pl.ds(MARKS[c], MARKS[c + 1] - MARKS[c]) for c in range(CHUNKS)]
    to_across = [
        remote(zsend.at[rows], zrecv.at[rows], z_send.at[c], z_recv.at[c], across) for c, rows in enumerate(chunk_rows)
    ]
    for c in range(AHEAD):
        to_across[c].start()
    for half in range(2):
        lanes = pl.ds(half * LANES, LANES)
        plane[1, pl.ds(half, BANDED, stride=2), :] = band[1, :, lanes]
    for c in range(AHEAD, CHUNKS):
        to_across[c - AHEAD].wait_send()
        to_across[c].start()

    lane = lax.broadcasted_iota(jnp.int32, (8, LANES), 1)

    def shift(d, keep, part):
        rows = {}

        def at(c):
            if c not in rows:
                values = plane[d, pl.ds(8 * QUAD * part + c, 8, stride=QUAD), :]
                rows[c] = values if keep is None else values * keep
            return rows[c]

        for i in range(4):
            for q in range(PARTS):
                for dx in range(-3, 4):
                    c, a = divmod(LEAD + NCOL * i + LANES * q + dx, LANES)
                    moved = at(c)
                    if a:
                        moved = pltpu.roll(jnp.where(lane >= a, moved, at(c + 1)), LANES - a, 1)
                    if q == 0 and dx < 0:
                        moved = jnp.where(lane >= -dx, moved, 0.0)
                    if q == PARTS - 1 and dx > 0:
                        moved = jnp.where(lane < NCOL - LANES * q - dx, moved, 0.0)
                    shifted[(d * 7 + dx + 3) * PARTS + q, pl.ds(32 * part + i, 8, stride=4), :] = moved

    def box(planes, t, q):
        sums = [None] * 2
        for d in planes:
            for dx in range(7):
                for dy in range(7):
                    e = d * 49 + dy * 7 + dx
                    weight = weights[e // 8 * PARTS + q, pl.ds(t * 64 + e % 8, 8, stride=8), :]
                    term = weight * shifted[(d * 7 + dx) * PARTS + q, pl.ds(t * 8 + dy, 8), :]
                    n = dx % 2
                    sums[n] = term if sums[n] is None else sums[n] + term
        return sums[0] + sums[1]

    def box_rows(planes, low, high, first):
        @pl.loop(low, high)
        def _(t):
            rows = pl.ds(pl.multiple_of(t * 8, 8), 8)
            for q in range(PARTS):
                total = box(planes, t, q)
                result[q, rows, :] = total if first else result[q, rows, :] + total

    def flatten(part):
        some = min(8, quads - 8 * part)
        pieces = [[] for _ in range(QUAD + 1)]
        for i in range(4):
            for q in range(PARTS):
                values = result[q, pl.ds(32 * part + i, some, stride=4), :]
                c, a = divmod(NCOL * i + LANES * q, LANES)
                end = a + min(LANES, NCOL - LANES * q)
                if a:
                    values = pltpu.roll(values, a, 1)
                pieces[c].append((a, values))
                if end > LANES:
                    pieces[c + 1].append((0, values))
        for c in range(QUAD):
            total = None
            for low, values in sorted(pieces[c], key=lambda piece: piece[0]):
                total = values if total is None else jnp.where(lane[0:some] >= low, values, total)
            out_ref[pl.ds(8 * QUAD * part + c, some, stride=QUAD), 0, :] = total

    to_sides = []
    for c in range(CHUNKS):
        rows = chunk_rows[c]
        to_across[c].wait_recv()
        plane[1, rows, :] = plane[1, rows, :] + zrecv[rows, :]
        to_sides.append(
            [
                remote(plane.at[1, rows], plane.at[target, rows], x_send.at[side, c], x_recv.at[side, c], device)
                for side, (target, device) in enumerate(((0, above), (2, below)))
            ]
        )
        for copy in to_sides[c]:
            copy.start()
        shift(1, None, c)
        box_rows((1,), BOX_MARKS[c], BOX_MARKS[c + 1], True)
    low_keep = (s > 0).astype(jnp.float32)
    high_keep = (s < slabs - 1).astype(jnp.float32)
    for c in range(CHUNKS):
        for copy in to_sides[c]:
            copy.wait_recv()
        shift(0, low_keep, c)
        shift(2, high_keep, c)
        box_rows((0, 2), BOX_MARKS[c], BOX_MARKS[c + 1], False)
        if c:
            flatten(c - 1)
    flatten(CHUNKS - 1)

    for copies in to_x + to_fwd + to_sides + [to_across[CHUNKS - AHEAD :], key_copies, [to_sibling]]:
        for copy in copies:
            copy.wait_send()


def per_device(tiles, lor_weight, block_map, kernel_weight):
    subsets, _, per_dev, lors, width = tiles.shape
    entries, planes, voxels = kernel_weight.shape
    plane_blocks = voxels * lax.axis_size("views") // width
    count = subsets * per_dev
    out_rows = voxels // LANES
    image_rows = voxels // NCOL
    groups = -(-entries // 8)
    hbm = pl.BlockSpec(memory_space=pl.ANY)
    vmem = pl.BlockSpec(memory_space=pltpu.VMEM)
    dma = pltpu.SemaphoreType.DMA
    out = pl.pallas_call(
        functools.partial(kernel, plane_blocks),
        out_shape=jax.ShapeDtypeStruct((out_rows, 1, LANES), jnp.float32),
        in_specs=[hbm, vmem, vmem, hbm],
        out_specs=vmem,
        scratch_shapes=[
            pltpu.VMEM((count * lors, width), jnp.bfloat16),
            pltpu.VMEM((RING, entries, QUAD * LANES), jnp.bfloat16),
            pltpu.VMEM((groups * PARTS, image_rows * 8, LANES), jnp.float32),
            pltpu.VMEM((6, count, width), jnp.float32),
            pltpu.VMEM((6, 8, 384), jnp.int32),
            pltpu.VMEM((2, BANDED, width), jnp.float32),
            pltpu.VMEM((ROWS, LANES), jnp.float32),
            pltpu.VMEM((ROWS, LANES), jnp.float32),
            pltpu.VMEM((3, ROWS + 8, LANES), jnp.float32),
            pltpu.VMEM((21 * PARTS, 128, LANES), jnp.float32),
            pltpu.VMEM((PARTS, 128, LANES), jnp.float32),
            dma((PIECES,)),
            dma((RING,)),
            dma((2, PIECES)),
            dma((2, PIECES)),
            dma((1,)),
            dma((1,)),
            dma((2, PIECES)),
            dma((2, PIECES)),
            dma((5,)),
            dma((5,)),
            dma((CHUNKS,)),
            dma((CHUNKS,)),
            dma((2, CHUNKS)),
            dma((2, CHUNKS)),
        ],
        compiler_params=pltpu.CompilerParams(
            collective_id=0, has_side_effects=True, vmem_limit_bytes=60 * 1024 * 1024
        ),
    )(
        tiles.reshape(count * lors, width),
        jnp.transpose(lor_weight.reshape(subsets, per_dev, lors), (0, 2, 1)),
        block_map.reshape(subsets, 1, per_dev),
        kernel_weight.reshape(entries, voxels),
    )
    return out.reshape(planes, voxels)


def solution(mesh):
    placed = (
        P(None, "slab", "views", None, None),
        P(None, "slab", "views", None),
        P(None, "slab", "views"),
        P(None, "slab", "views"),
    )
    return jax.shard_map(
        per_device, mesh=mesh, in_specs=placed, out_specs=P("slab", "views"), check_vma=False
    )
```

```python
import functools

import jax
import jax.numpy as jnp
from jax import lax
from jax.experimental import pallas as pl
from jax.experimental.pallas import tpu as pltpu
from jax.sharding import PartitionSpec as P

MESH = pl.DeviceIdType.MESH
NCOL = 480
LANES = 128
BLOCK = 256
HALO = 6
BANDED = 240
ROWS = 2 * BANDED
LEAD = HALO * BLOCK - 3 * NCOL
QUAD = 4 * NCOL // LANES
PARTS = 4
MARKS = (0, 128, 248, 368, ROWS)
CHUNKS = len(MARKS) - 1
BOX_MARKS = (0, 3, 7, 11, 15)
PIECES = 4
AHEAD = 2
RING = 4


def kernel(
    plane_blocks, tiles_hbm, lor_ref, map_ref, kw_hbm, out_ref,
    tiles, raw, stage, weights, contrib, keys, band, zsend, zrecv, plane, shifted, result,
    tile_sem, raw_sem, raw_send, raw_recv, sib_send, sib_recv, fwd_send, fwd_recv, key_send, key_recv,
    z_send, z_recv, x_send, x_recv,
):
    subsets, lors, per_dev = lor_ref.shape
    entries, voxels = kw_hbm.shape
    count = subsets * per_dev
    piece = count // PIECES
    band_blocks = voxels // BLOCK
    quads = voxels // (QUAD * LANES)
    pairs = quads // 2

    v = lax.axis_index("views")
    s = lax.axis_index("slab")
    slabs = lax.axis_size("slab")
    sibling = (v // 2 * 2 + 1 - lax.rem(v, 2), s)
    opposite = lax.rem(v + 2, 4)
    across = (opposite, s)
    above = (v, lax.rem(s + 1, slabs))
    below = (v, lax.rem(s + slabs - 1, slabs))

    has_above = s < slabs - 1
    has_below = s > 0

    barrier = pltpu.get_barrier_semaphore()

    def greet(device):
        pl.semaphore_signal(barrier, inc=1, device_id=device, device_id_type=MESH)

    greet(sibling)
    greet(across)
    pl.when(has_above)(lambda: greet(above))
    pl.when(has_below)(lambda: greet(below))

    class Copy:
        def __init__(self, src, dst, send, recv, device, there=None, here=None):
            self.there, self.here = there, here
            self.copy = pltpu.make_async_remote_copy(
                src_ref=src, dst_ref=dst, send_sem=send, recv_sem=recv, device_id=device, device_id_type=MESH
            )

        def on(self, condition, step):
            if condition is None:
                step()
            else:
                pl.when(condition)(step)

        def start(self):
            self.on(self.there, self.copy.start)

        def wait_send(self):
            self.on(self.there, self.copy.wait_send)

        def wait_recv(self):
            self.on(self.here, self.copy.wait_recv)

    piece_rows = piece * lors
    tile_loads = [
        pltpu.make_async_copy(
            tiles_hbm.at[pl.ds(n * piece_rows, piece_rows)], tiles.at[pl.ds(n * piece_rows, piece_rows)], tile_sem.at[n]
        )
        for n in range(PIECES)
    ]
    for load in tile_loads:
        load.start()

    def raw_load(m, slot):
        lanes = 2 * QUAD * LANES
        start = m * lanes if isinstance(m, int) else pl.multiple_of(m * lanes, lanes)
        return pltpu.make_async_copy(kw_hbm.at[:, pl.ds(start, lanes)], raw.at[slot], raw_sem.at[slot])

    for m in range(RING):
        raw_load(m, m).start()

    def sides(for_above, for_below):
        return ((for_above, above, has_above, has_below), (for_below, below, has_below, has_above))

    to_x, to_fwd, key_copies = [], [], []
    for n in range(PIECES):
        rows = pl.ds(n * piece, piece)
        pair = []
        for side, (target, device, there, here) in enumerate(sides(1, 2)):
            pair.append(
                Copy(
                    contrib.at[0, rows], contrib.at[target, rows], raw_send.at[side, n], raw_recv.at[side, n],
                    device, there, here,
                )
            )
        to_x.append(pair)
        to_fwd.append(
            [
                Copy(
                    contrib.at[side + 1, rows], contrib.at[side + 4, rows],
                    fwd_send.at[side, n], fwd_recv.at[side, n], sibling, has, has,
                )
                for side, has in enumerate((has_below, has_above))
            ]
        )
    for n, (source, target, device, there, here) in enumerate(
        (
            (0, 1, above, has_above, has_below),
            (0, 2, below, has_below, has_above),
            (0, 3, sibling, None, None),
            (1, 4, sibling, has_below, has_below),
            (2, 5, sibling, has_above, has_above),
        )
    ):
        key_copies.append(
            Copy(keys.at[source], keys.at[target], key_send.at[n], key_recv.at[n], device, there, here)
        )
    to_sibling = Copy(contrib.at[0], contrib.at[3], sib_send.at[0], sib_recv.at[0], sibling)

    def nothing(plane_at, sets):
        plane[plane_at] = jnp.zeros(plane.shape[1:], jnp.float32)
        for index in sets:
            contrib[index] = jnp.zeros(contrib.shape[1:], jnp.float32)
            keys[index] = jnp.full(keys.shape[1:], -1, jnp.int32)

    pl.when(jnp.logical_not(has_below))(lambda: nothing(0, (1, 4)))
    pl.when(jnp.logical_not(has_above))(lambda: nothing(2, (2, 5)))

    width = keys.shape[2]
    pad = jnp.full((1, width - count), -1, jnp.int32)
    row = jnp.concatenate([map_ref[u] for u in range(subsets)] + [pad], axis=1)
    keys[0] = jnp.broadcast_to(row, keys.shape[1:])
    spread = (
        lax.rem(lax.broadcasted_iota(jnp.int32, (lors, BLOCK), 1), lors)
        == lax.broadcasted_iota(jnp.int32, (lors, BLOCK), 0)
    ).astype(jnp.float32).astype(jnp.bfloat16)
    group = BLOCK // lors
    diagonal = (
        lax.rem(lax.broadcasted_iota(jnp.int32, (per_dev, BLOCK), 0), group)
        == lax.broadcasted_iota(jnp.int32, (per_dev, BLOCK), 1) // lors
    )
    wide = []
    for u in range(subsets):
        spread_out = lax.dot_general(
            lor_ref[u], spread, (((0,), (0,)), ((), ())), preferred_element_type=jnp.float32
        )
        wide.append(jnp.where(diagonal, spread_out, 0.0).astype(jnp.bfloat16))
    for n in range(PIECES):
        tile_loads[n].wait()
        for first in range(n * piece, (n + 1) * piece, group):
            own = first % per_dev
            contrib[0, pl.ds(first, group), :] = jnp.dot(
                wide[first // per_dev][own : own + group], tiles[pl.ds(first * lors, BLOCK), :],
                preferred_element_type=jnp.float32,
            )
        if n == 0:
            pl.semaphore_wait(barrier, 2 + has_above.astype(jnp.int32) + has_below.astype(jnp.int32))
            for k in range(3):
                key_copies[k].start()
        if n < AHEAD:
            for copy in to_x[n]:
                copy.start()
    to_sibling.start()

    lane16 = lax.broadcasted_iota(jnp.int32, (16, LANES), 1)

    def turn(slot, m):
        for base in range(0, entries, 16):
            size = min(16, entries - base)
            for quad in range(2):
                here = [raw[slot, pl.ds(base, size), pl.ds((quad * QUAD + c) * LANES, LANES)] for c in range(QUAD)]
                for i in range(4):
                    first, a = divmod(NCOL * i, LANES)
                    for q in range(PARTS):
                        values = here[first + q]
                        if a:
                            if first + q + 1 < QUAD:
                                values = jnp.where(lane16[0:size] >= a, values, here[first + q + 1])
                            values = pltpu.roll(values, LANES - a, 1)
                        values = values.astype(jnp.float32)
                        for half in range(0, size, 8):
                            some = min(8, size - half)
                            stage[(base + half) // 8 * PARTS + q, pl.ds((4 * quad + i) * 8, some), :] = values[
                                half : half + some
                            ]
            for e in range(base, base + size):
                for q in range(PARTS):
                    block = e // 8 * PARTS + q
                    weights[block, pl.ds(pl.multiple_of(m * 64 + e % 8 * 8, 8), 8), :] = stage[
                        block, pl.ds(e % 8, 8, stride=8), :
                    ]

    def turn_pairs(low, high):
        @pl.loop(low, high)
        def _(m):
            slot = lax.rem(m, RING)
            raw_load(m, slot).wait()
            turn(slot, m)

            @pl.when(m + RING < pairs)
            def _():
                raw_load(m + RING, slot).start()

    def scatter(sets, into, first):
        for index in sets:
            delta = (0, -1, 1)[index % 3]
            whole = contrib[index]
            high = whole.astype(jnp.bfloat16)
            low = (whole - high.astype(jnp.float32)).astype(jnp.bfloat16)
            place = keys[index][0:1, 0:count] - plane_blocks * (1 - delta)
            inside = (place >= 0) & (place < plane_blocks)
            for n, view in enumerate((opposite, v)):
                target = jnp.where(inside, place - (band_blocks * view - HALO), -1)
                chosen = lax.broadcasted_iota(jnp.int32, (BANDED, count), 0) == target
                chosen = jnp.where(chosen, 1.0, 0.0).astype(jnp.bfloat16)
                total = jnp.dot(chosen, high, preferred_element_type=jnp.float32) + jnp.dot(
                    chosen, low, preferred_element_type=jnp.float32
                )
                if first and index == sets[0]:
                    into[n] = total
                else:
                    into[n] = into[n] + total

    turn_pairs(0, pairs // 3)
    for n in range(AHEAD, PIECES):
        for copy in to_x[n]:
            copy.start()
    turn_pairs(pairs // 3, pairs * 2 // 3)
    for k in range(2):
        key_copies[k].wait_recv()
        key_copies[3 + k].start()
    for n in range(AHEAD):
        for side in range(2):
            to_x[n][side].wait_recv()
            to_fwd[n][side].start()
    turn_pairs(pairs * 2 // 3, pairs)
    for n in range(AHEAD, PIECES):
        for side in range(2):
            to_x[n][side].wait_recv()
            to_fwd[n][side].start()
    key_copies[2].wait_recv()
    to_sibling.wait_recv()
    scatter((0, 3, 1, 2), band, True)
    for k in range(2):
        key_copies[3 + k].wait_recv()
    for n in range(PIECES):
        for side in range(2):
            to_fwd[n][side].wait_recv()
    scatter((4, 5), band, False)

    for half in range(2):
        lanes = pl.ds(half * LANES, LANES)
        zsend[pl.ds(half, BANDED, stride=2), :] = band[0, :, lanes]
    chunk_rows = [pl.ds(MARKS[c], MARKS[c + 1] - MARKS[c]) for c in range(CHUNKS)]
    to_across = [
        Copy(zsend.at[rows], zrecv.at[rows], z_send.at[c], z_recv.at[c], across) for c, rows in enumerate(chunk_rows)
    ]
    for c in range(AHEAD):
        to_across[c].start()
    for half in range(2):
        lanes = pl.ds(half * LANES, LANES)
        plane[1, pl.ds(half, BANDED, stride=2), :] = band[1, :, lanes]
    for c in range(AHEAD, CHUNKS):
        to_across[c - AHEAD].wait_send()
        to_across[c].start()

    lane = lax.broadcasted_iota(jnp.int32, (8, LANES), 1)

    def shift(d, part):
        rows = {}

        def at(c):
            if c not in rows:
                rows[c] = plane[d, pl.ds(8 * QUAD * part + c, 8, stride=QUAD), :]
            return rows[c]

        for i in range(4):
            for q in range(PARTS):
                for dx in range(-3, 4):
                    c, a = divmod(LEAD + NCOL * i + LANES * q + dx, LANES)
                    moved = at(c)
                    if a:
                        moved = pltpu.roll(jnp.where(lane >= a, moved, at(c + 1)), LANES - a, 1)
                    if q == 0 and dx < 0:
                        moved = jnp.where(lane >= -dx, moved, 0.0)
                    if q == PARTS - 1 and dx > 0:
                        moved = jnp.where(lane < NCOL - LANES * q - dx, moved, 0.0)
                    shifted[(d * 7 + dx + 3) * PARTS + q, pl.ds(32 * part + i, 8, stride=4), :] = moved

    def box(planes, t, q):
        sums = [None] * 2
        for d in planes:
            for dx in range(7):
                for dy in range(7):
                    e = d * 49 + dy * 7 + dx
                    weight = weights[e // 8 * PARTS + q, pl.ds(pl.multiple_of(t * 64 + e % 8 * 8, 8), 8), :]
                    term = weight * shifted[(d * 7 + dx) * PARTS + q, pl.ds(t * 8 + dy, 8), :]
                    n = dx % 2
                    sums[n] = term if sums[n] is None else sums[n] + term
        return sums[0] + sums[1]

    def box_rows(planes, low, high, first):
        @pl.loop(low, high)
        def _(t):
            rows = pl.ds(pl.multiple_of(t * 8, 8), 8)
            for q in range(PARTS):
                total = box(planes, t, q)
                result[q, rows, :] = total if first else result[q, rows, :] + total

    def flatten(part):
        some = min(8, quads - 8 * part)
        pieces = [[] for _ in range(QUAD + 1)]
        for i in range(4):
            for q in range(PARTS):
                values = result[q, pl.ds(32 * part + i, some, stride=4), :]
                c, a = divmod(NCOL * i + LANES * q, LANES)
                end = a + min(LANES, NCOL - LANES * q)
                if a:
                    values = pltpu.roll(values, a, 1)
                pieces[c].append((a, values))
                if end > LANES:
                    pieces[c + 1].append((0, values))
        for c in range(QUAD):
            total = None
            for low, values in sorted(pieces[c], key=lambda piece: piece[0]):
                total = values if total is None else jnp.where(lane[0:some] >= low, values, total)
            out_ref[pl.ds(8 * QUAD * part + c, some, stride=QUAD), 0, :] = total

    to_sides = []
    for c in range(CHUNKS):
        rows = chunk_rows[c]
        to_across[c].wait_recv()
        plane[1, rows, :] = plane[1, rows, :] + zrecv[rows, :]
        to_sides.append(
            [
                Copy(
                    plane.at[1, rows], plane.at[target, rows], x_send.at[side, c], x_recv.at[side, c],
                    device, there, here,
                )
                for side, (target, device, there, here) in enumerate(sides(0, 2))
            ]
        )
        for copy in to_sides[c]:
            copy.start()
        shift(1, c)
        box_rows((1,), BOX_MARKS[c], BOX_MARKS[c + 1], True)
    for c in range(CHUNKS):
        for copy in to_sides[c]:
            copy.wait_recv()
        shift(0, c)
        shift(2, c)
        box_rows((0, 2), BOX_MARKS[c], BOX_MARKS[c + 1], False)
        if c:
            flatten(c - 1)
    flatten(CHUNKS - 1)

    for copies in to_x + to_fwd + to_sides + [to_across[CHUNKS - AHEAD :], key_copies, [to_sibling]]:
        for copy in copies:
            copy.wait_send()


def per_device(tiles, lor_weight, block_map, kernel_weight):
    subsets, _, per_dev, lors, width = tiles.shape
    entries, planes, voxels = kernel_weight.shape
    plane_blocks = voxels * lax.axis_size("views") // width
    count = subsets * per_dev
    out_rows = voxels // LANES
    image_rows = voxels // NCOL
    groups = -(-entries // 8)
    hbm = pl.BlockSpec(memory_space=pl.ANY)
    vmem = pl.BlockSpec(memory_space=pltpu.VMEM)
    dma = pltpu.SemaphoreType.DMA
    out = pl.pallas_call(
        functools.partial(kernel, plane_blocks),
        out_shape=jax.ShapeDtypeStruct((out_rows, 1, LANES), jnp.float32),
        in_specs=[hbm, vmem, vmem, hbm],
        out_specs=vmem,
        scratch_shapes=[
            pltpu.VMEM((count * lors, width), jnp.bfloat16),
            pltpu.VMEM((RING, entries, 2 * QUAD * LANES), jnp.bfloat16),
            pltpu.VMEM((groups * PARTS, 64, LANES), jnp.float32),
            pltpu.VMEM((groups * PARTS, image_rows * 8, LANES), jnp.float32),
            pltpu.VMEM((6, count, width), jnp.float32),
            pltpu.VMEM((6, 8, 384), jnp.int32),
            pltpu.VMEM((2, BANDED, width), jnp.float32),
            pltpu.VMEM((ROWS, LANES), jnp.float32),
            pltpu.VMEM((ROWS, LANES), jnp.float32),
            pltpu.VMEM((3, ROWS + 8, LANES), jnp.float32),
            pltpu.VMEM((21 * PARTS, 128, LANES), jnp.float32),
            pltpu.VMEM((PARTS, 128, LANES), jnp.float32),
            dma((PIECES,)),
            dma((RING,)),
            dma((2, PIECES)),
            dma((2, PIECES)),
            dma((1,)),
            dma((1,)),
            dma((2, PIECES)),
            dma((2, PIECES)),
            dma((5,)),
            dma((5,)),
            dma((CHUNKS,)),
            dma((CHUNKS,)),
            dma((2, CHUNKS)),
            dma((2, CHUNKS)),
        ],
        compiler_params=pltpu.CompilerParams(
            collective_id=0, has_side_effects=True, vmem_limit_bytes=60 * 1024 * 1024
        ),
    )(
        tiles.reshape(count * lors, width),
        jnp.transpose(lor_weight.reshape(subsets, per_dev, lors), (0, 2, 1)),
        block_map.reshape(subsets, 1, per_dev),
        kernel_weight.reshape(entries, voxels),
    )
    return out.reshape(planes, voxels)


def solution(mesh):
    placed = (
        P(None, "slab", "views", None, None),
        P(None, "slab", "views", None),
        P(None, "slab", "views"),
        P(None, "slab", "views"),
    )
    return jax.shard_map(
        per_device, mesh=mesh, in_specs=placed, out_specs=P("slab", "views"), check_vma=False
    )
```

```python
import functools

import jax
import jax.numpy as jnp
from jax import lax
from jax.experimental import pallas as pl
from jax.experimental.pallas import tpu as pltpu
from jax.sharding import PartitionSpec as P

MESH = pl.DeviceIdType.MESH
NCOL = 480
LANES = 128
BLOCK = 256
HALO = 6
BANDED = 240
ROWS = 2 * BANDED
LEAD = HALO * BLOCK - 3 * NCOL
QUAD = 4 * NCOL // LANES
PARTS = 4
MARKS = (0, 128, 248, 368, ROWS)
CHUNKS = len(MARKS) - 1
BOX_MARKS = (0, 3, 7, 11, 15)
PIECES = 4
AHEAD = 2
RING = 4


def kernel(
    plane_blocks, tiles_hbm, lor_ref, map_ref, kw_hbm, out_ref,
    tiles, raw, stage, weights, contrib, keys, band, zsend, zrecv, plane, shifted, result,
    tile_sem, raw_sem, raw_send, raw_recv, sib_send, sib_recv, fwd_send, fwd_recv, key_send, key_recv,
    z_send, z_recv, x_send, x_recv,
):
    subsets, lors, per_dev = lor_ref.shape
    entries, voxels = kw_hbm.shape
    count = subsets * per_dev
    piece = count // PIECES
    band_blocks = voxels // BLOCK
    quads = voxels // (QUAD * LANES)
    pairs = quads // 2

    v = lax.axis_index("views")
    s = lax.axis_index("slab")
    slabs = lax.axis_size("slab")
    sibling = (v // 2 * 2 + 1 - lax.rem(v, 2), s)
    opposite = lax.rem(v + 2, 4)
    across = (opposite, s)
    above = (v, lax.rem(s + 1, slabs))
    below = (v, lax.rem(s + slabs - 1, slabs))

    has_above = s < slabs - 1
    has_below = s > 0

    barrier = pltpu.get_barrier_semaphore()

    def greet(device):
        pl.semaphore_signal(barrier, inc=1, device_id=device, device_id_type=MESH)

    greet(sibling)
    greet(across)
    pl.when(has_above)(lambda: greet(above))
    pl.when(has_below)(lambda: greet(below))

    class Copy:
        def __init__(self, src, dst, send, recv, device, there=None, here=None):
            self.there, self.here = there, here
            self.copy = pltpu.make_async_remote_copy(
                src_ref=src, dst_ref=dst, send_sem=send, recv_sem=recv, device_id=device, device_id_type=MESH
            )

        def on(self, condition, step):
            if condition is None:
                step()
            else:
                pl.when(condition)(step)

        def start(self):
            self.on(self.there, self.copy.start)

        def wait_send(self):
            self.on(self.there, self.copy.wait_send)

        def wait_recv(self):
            self.on(self.here, self.copy.wait_recv)

    piece_rows = piece * lors
    tile_loads = [
        pltpu.make_async_copy(
            tiles_hbm.at[pl.ds(n * piece_rows, piece_rows)], tiles.at[pl.ds(n * piece_rows, piece_rows)], tile_sem.at[n]
        )
        for n in range(PIECES)
    ]
    for load in tile_loads:
        load.start()

    def raw_load(m, slot):
        lanes = 2 * QUAD * LANES
        start = m * lanes if isinstance(m, int) else pl.multiple_of(m * lanes, lanes)
        return pltpu.make_async_copy(kw_hbm.at[:, pl.ds(start, lanes)], raw.at[slot], raw_sem.at[slot])

    for m in range(RING):
        raw_load(m, m).start()

    def sides(for_above, for_below):
        return ((for_above, above, has_above, has_below), (for_below, below, has_below, has_above))

    to_x, to_fwd, key_copies = [], [], []
    for n in range(PIECES):
        rows = pl.ds(n * piece, piece)
        pair = []
        for side, (target, device, there, here) in enumerate(sides(1, 2)):
            pair.append(
                Copy(
                    contrib.at[0, rows], contrib.at[target, rows], raw_send.at[side, n], raw_recv.at[side, n],
                    device, there, here,
                )
            )
        to_x.append(pair)
        to_fwd.append(
            [
                Copy(
                    contrib.at[side + 1, rows], contrib.at[side + 4, rows],
                    fwd_send.at[side, n], fwd_recv.at[side, n], sibling, has, has,
                )
                for side, has in enumerate((has_below, has_above))
            ]
        )
    for n, (source, target, device, there, here) in enumerate(
        (
            (0, 1, above, has_above, has_below),
            (0, 2, below, has_below, has_above),
            (0, 3, sibling, None, None),
            (1, 4, sibling, has_below, has_below),
            (2, 5, sibling, has_above, has_above),
        )
    ):
        key_copies.append(
            Copy(keys.at[source], keys.at[target], key_send.at[n], key_recv.at[n], device, there, here)
        )
    to_sibling = Copy(contrib.at[0], contrib.at[3], sib_send.at[0], sib_recv.at[0], sibling)

    def nothing(plane_at, sets):
        plane[plane_at] = jnp.zeros(plane.shape[1:], jnp.float32)
        for index in sets:
            contrib[index] = jnp.zeros(contrib.shape[1:], jnp.float32)
            keys[index] = jnp.full(keys.shape[1:], -1, jnp.int32)

    pl.when(jnp.logical_not(has_below))(lambda: nothing(0, (1, 4)))
    pl.when(jnp.logical_not(has_above))(lambda: nothing(2, (2, 5)))

    width = keys.shape[2]
    pad = jnp.full((1, width - count), -1, jnp.int32)
    row = jnp.concatenate([map_ref[u] for u in range(subsets)] + [pad], axis=1)
    keys[0] = jnp.broadcast_to(row, keys.shape[1:])
    spread = (
        lax.rem(lax.broadcasted_iota(jnp.int32, (lors, BLOCK), 1), lors)
        == lax.broadcasted_iota(jnp.int32, (lors, BLOCK), 0)
    ).astype(jnp.float32).astype(jnp.bfloat16)
    group = BLOCK // lors
    diagonal = (
        lax.rem(lax.broadcasted_iota(jnp.int32, (per_dev, BLOCK), 0), group)
        == lax.broadcasted_iota(jnp.int32, (per_dev, BLOCK), 1) // lors
    )
    wide = []
    for u in range(subsets):
        spread_out = lax.dot_general(
            lor_ref[u], spread, (((0,), (0,)), ((), ())), preferred_element_type=jnp.float32
        )
        wide.append(jnp.where(diagonal, spread_out, 0.0).astype(jnp.bfloat16))
    for n in range(PIECES):
        tile_loads[n].wait()
        for first in range(n * piece, (n + 1) * piece, group):
            own = first % per_dev
            contrib[0, pl.ds(first, group), :] = jnp.dot(
                wide[first // per_dev][own : own + group], tiles[pl.ds(first * lors, BLOCK), :],
                preferred_element_type=jnp.float32,
            )
        if n == 0:
            pl.semaphore_wait(barrier, 2 + has_above.astype(jnp.int32) + has_below.astype(jnp.int32))
            for k in range(3):
                key_copies[k].start()
        if n < AHEAD:
            for copy in to_x[n]:
                copy.start()
    lane16 = lax.broadcasted_iota(jnp.int32, (16, LANES), 1)

    def turn(slot, m):
        for base in range(0, entries, 16):
            size = min(16, entries - base)
            for quad in range(2):
                here = [raw[slot, pl.ds(base, size), pl.ds((quad * QUAD + c) * LANES, LANES)] for c in range(QUAD)]
                for i in range(4):
                    first, a = divmod(NCOL * i, LANES)
                    for q in range(PARTS):
                        values = here[first + q]
                        if a:
                            if first + q + 1 < QUAD:
                                values = jnp.where(lane16[0:size] >= a, values, here[first + q + 1])
                            values = pltpu.roll(values, LANES - a, 1)
                        values = values.astype(jnp.float32)
                        for half in range(0, size, 8):
                            some = min(8, size - half)
                            stage[(base + half) // 8 * PARTS + q, pl.ds((4 * quad + i) * 8, some), :] = values[
                                half : half + some
                            ]
            for e in range(base, base + size, 2):
                for q in range(PARTS):
                    block = e // 8 * PARTS + q
                    both = [stage[block, pl.ds(min(e + n, entries - 1) % 8, 8, stride=8), :] for n in range(2)]
                    weights[block, pl.ds(pl.multiple_of(m * 64 + e % 8 * 8, 16), 16), :] = jnp.concatenate(
                        both, axis=0
                    ).astype(jnp.bfloat16)

    def turn_pairs(low, high):
        @pl.loop(low, high)
        def _(m):
            slot = lax.rem(m, RING)
            raw_load(m, slot).wait()
            turn(slot, m)

            @pl.when(m + RING < pairs)
            def _():
                raw_load(m + RING, slot).start()

    def scatter(sets, into, first):
        for index in sets:
            delta = (0, -1, 1)[index % 3]
            whole = contrib[index]
            high = whole.astype(jnp.bfloat16)
            low = (whole - high.astype(jnp.float32)).astype(jnp.bfloat16)
            place = keys[index][0:1, 0:count] - plane_blocks * (1 - delta)
            inside = (place >= 0) & (place < plane_blocks)
            for n, view in enumerate((opposite, v)):
                target = jnp.where(inside, place - (band_blocks * view - HALO), -1)
                chosen = lax.broadcasted_iota(jnp.int32, (BANDED, count), 0) == target
                chosen = jnp.where(chosen, 1.0, 0.0).astype(jnp.bfloat16)
                total = jnp.dot(chosen, high, preferred_element_type=jnp.float32) + jnp.dot(
                    chosen, low, preferred_element_type=jnp.float32
                )
                if first and index == sets[0]:
                    into[n] = total
                else:
                    into[n] = into[n] + total

    turn_pairs(0, pairs // 3)
    for n in range(AHEAD, PIECES):
        for copy in to_x[n]:
            copy.start()
    to_sibling.start()
    turn_pairs(pairs // 3, pairs * 2 // 3)
    for k in range(2):
        key_copies[k].wait_recv()
        key_copies[3 + k].start()
    for n in range(AHEAD):
        for side in range(2):
            to_x[n][side].wait_recv()
            to_fwd[n][side].start()
    turn_pairs(pairs * 2 // 3, pairs)
    for n in range(AHEAD, PIECES):
        for side in range(2):
            to_x[n][side].wait_recv()
            to_fwd[n][side].start()
    key_copies[2].wait_recv()
    to_sibling.wait_recv()
    scatter((0, 3, 1, 2), band, True)
    for k in range(2):
        key_copies[3 + k].wait_recv()
    for n in range(PIECES):
        for side in range(2):
            to_fwd[n][side].wait_recv()
    scatter((4, 5), band, False)

    for half in range(2):
        lanes = pl.ds(half * LANES, LANES)
        zsend[pl.ds(half, BANDED, stride=2), :] = band[0, :, lanes]
    chunk_rows = [pl.ds(MARKS[c], MARKS[c + 1] - MARKS[c]) for c in range(CHUNKS)]
    to_across = [
        Copy(zsend.at[rows], zrecv.at[rows], z_send.at[c], z_recv.at[c], across) for c, rows in enumerate(chunk_rows)
    ]
    for c in range(AHEAD):
        to_across[c].start()
    for half in range(2):
        lanes = pl.ds(half * LANES, LANES)
        plane[1, pl.ds(half, BANDED, stride=2), :] = band[1, :, lanes]
    for c in range(AHEAD, CHUNKS):
        to_across[c - AHEAD].wait_send()
        to_across[c].start()

    lane = lax.broadcasted_iota(jnp.int32, (8, LANES), 1)

    def shift(d, part):
        rows = {}

        def at(c):
            if c not in rows:
                rows[c] = plane[d, pl.ds(8 * QUAD * part + c, 8, stride=QUAD), :]
            return rows[c]

        for i in range(4):
            for q in range(PARTS):
                for dx in range(-3, 4):
                    c, a = divmod(LEAD + NCOL * i + LANES * q + dx, LANES)
                    moved = at(c)
                    if a:
                        moved = pltpu.roll(jnp.where(lane >= a, moved, at(c + 1)), LANES - a, 1)
                    if q == 0 and dx < 0:
                        moved = jnp.where(lane >= -dx, moved, 0.0)
                    if q == PARTS - 1 and dx > 0:
                        moved = jnp.where(lane < NCOL - LANES * q - dx, moved, 0.0)
                    shifted[(d * 7 + dx + 3) * PARTS + q, pl.ds(32 * part + i, 8, stride=4), :] = moved

    def box(planes, t, q):
        sums = [None] * 2
        for pair in range(0, entries, 2):
            wanted = [e for e in (pair, pair + 1) if e < entries and e // 49 in planes]
            if not wanted:
                continue
            both = weights[
                pair // 8 * PARTS + q, pl.ds(pl.multiple_of(t * 64 + pair % 8 * 8, 16), 16), :
            ].astype(jnp.float32)
            for e in wanted:
                d, dy, dx = e // 49, e // 7 % 7, e % 7
                n = e % 2
                term = both[8 * n : 8 * n + 8] * shifted[(d * 7 + dx) * PARTS + q, pl.ds(t * 8 + dy, 8), :]
                sums[n] = term if sums[n] is None else sums[n] + term
        return sums[0] + sums[1]

    def box_rows(planes, low, high, first):
        @pl.loop(low, high)
        def _(t):
            rows = pl.ds(pl.multiple_of(t * 8, 8), 8)
            for q in range(PARTS):
                total = box(planes, t, q)
                result[q, rows, :] = total if first else result[q, rows, :] + total

    def flatten(part):
        some = min(8, quads - 8 * part)
        pieces = [[] for _ in range(QUAD + 1)]
        for i in range(4):
            for q in range(PARTS):
                values = result[q, pl.ds(32 * part + i, some, stride=4), :]
                c, a = divmod(NCOL * i + LANES * q, LANES)
                end = a + min(LANES, NCOL - LANES * q)
                if a:
                    values = pltpu.roll(values, a, 1)
                pieces[c].append((a, values))
                if end > LANES:
                    pieces[c + 1].append((0, values))
        for c in range(QUAD):
            total = None
            for low, values in sorted(pieces[c], key=lambda piece: piece[0]):
                total = values if total is None else jnp.where(lane[0:some] >= low, values, total)
            out_ref[pl.ds(8 * QUAD * part + c, some, stride=QUAD), 0, :] = total

    to_sides = []
    for c in range(CHUNKS):
        rows = chunk_rows[c]
        to_across[c].wait_recv()
        plane[1, rows, :] = plane[1, rows, :] + zrecv[rows, :]
        to_sides.append(
            [
                Copy(
                    plane.at[1, rows], plane.at[target, rows], x_send.at[side, c], x_recv.at[side, c],
                    device, there, here,
                )
                for side, (target, device, there, here) in enumerate(sides(0, 2))
            ]
        )
        for copy in to_sides[c]:
            copy.start()
        shift(1, c)
        box_rows((1,), BOX_MARKS[c], BOX_MARKS[c + 1], True)
    for c in range(CHUNKS):
        for copy in to_sides[c]:
            copy.wait_recv()
        shift(0, c)
        shift(2, c)
        box_rows((0, 2), BOX_MARKS[c], BOX_MARKS[c + 1], False)
        if c:
            flatten(c - 1)
    flatten(CHUNKS - 1)

    for copies in to_x + to_fwd + to_sides + [to_across[CHUNKS - AHEAD :], key_copies, [to_sibling]]:
        for copy in copies:
            copy.wait_send()


def per_device(tiles, lor_weight, block_map, kernel_weight):
    subsets, _, per_dev, lors, width = tiles.shape
    entries, planes, voxels = kernel_weight.shape
    plane_blocks = voxels * lax.axis_size("views") // width
    count = subsets * per_dev
    out_rows = voxels // LANES
    image_rows = voxels // NCOL
    groups = -(-entries // 8)
    hbm = pl.BlockSpec(memory_space=pl.ANY)
    vmem = pl.BlockSpec(memory_space=pltpu.VMEM)
    dma = pltpu.SemaphoreType.DMA
    out = pl.pallas_call(
        functools.partial(kernel, plane_blocks),
        out_shape=jax.ShapeDtypeStruct((out_rows, 1, LANES), jnp.float32),
        in_specs=[hbm, vmem, vmem, hbm],
        out_specs=vmem,
        scratch_shapes=[
            pltpu.VMEM((count * lors, width), jnp.bfloat16),
            pltpu.VMEM((RING, entries, 2 * QUAD * LANES), jnp.bfloat16),
            pltpu.VMEM((groups * PARTS, 64, LANES), jnp.float32),
            pltpu.VMEM((groups * PARTS, image_rows * 8, LANES), jnp.bfloat16),
            pltpu.VMEM((6, count, width), jnp.float32),
            pltpu.VMEM((6, 8, 384), jnp.int32),
            pltpu.VMEM((2, BANDED, width), jnp.float32),
            pltpu.VMEM((ROWS, LANES), jnp.float32),
            pltpu.VMEM((ROWS, LANES), jnp.float32),
            pltpu.VMEM((3, ROWS + 8, LANES), jnp.float32),
            pltpu.VMEM((21 * PARTS, 128, LANES), jnp.float32),
            pltpu.VMEM((PARTS, 128, LANES), jnp.float32),
            dma((PIECES,)),
            dma((RING,)),
            dma((2, PIECES)),
            dma((2, PIECES)),
            dma((1,)),
            dma((1,)),
            dma((2, PIECES)),
            dma((2, PIECES)),
            dma((5,)),
            dma((5,)),
            dma((CHUNKS,)),
            dma((CHUNKS,)),
            dma((2, CHUNKS)),
            dma((2, CHUNKS)),
        ],
        compiler_params=pltpu.CompilerParams(
            collective_id=0, has_side_effects=True, vmem_limit_bytes=60 * 1024 * 1024
        ),
    )(
        tiles.reshape(count * lors, width),
        jnp.transpose(lor_weight.reshape(subsets, per_dev, lors), (0, 2, 1)),
        block_map.reshape(subsets, 1, per_dev),
        kernel_weight.reshape(entries, voxels),
    )
    return out.reshape(planes, voxels)


def solution(mesh):
    placed = (
        P(None, "slab", "views", None, None),
        P(None, "slab", "views", None),
        P(None, "slab", "views"),
        P(None, "slab", "views"),
    )
    return jax.shard_map(
        per_device, mesh=mesh, in_specs=placed, out_specs=P("slab", "views"), check_vma=False
    )
```

```python
import functools

import jax
import jax.numpy as jnp
from jax import lax
from jax.experimental import pallas as pl
from jax.experimental.pallas import tpu as pltpu
from jax.sharding import PartitionSpec as P

MESH = pl.DeviceIdType.MESH
NCOL = 480
LANES = 128
BLOCK = 256
HALO = 6
BANDED = 240
ROWS = 2 * BANDED
LEAD = HALO * BLOCK - 3 * NCOL
QUAD = 4 * NCOL // LANES
PARTS = 4
MARKS = (0, 128, 248, 368, ROWS)
CHUNKS = len(MARKS) - 1
BOX_MARKS = (0, 3, 7, 11, 15)
PIECES = 4
AHEAD = 2
RING = 4


def kernel(
    plane_blocks, tiles_hbm, lor_ref, map_ref, kw_hbm, out_ref,
    tiles, raw, stage, weights, contrib, keys, band, zsend, zrecv, plane, shifted, result,
    tile_sem, raw_sem, raw_send, raw_recv, sib_send, sib_recv, fwd_send, fwd_recv, key_send, key_recv,
    z_send, z_recv, x_send, x_recv,
):
    subsets, lors, per_dev = lor_ref.shape
    entries, voxels = kw_hbm.shape
    count = subsets * per_dev
    piece = count // PIECES
    band_blocks = voxels // BLOCK
    quads = voxels // (QUAD * LANES)
    pairs = quads // 2

    v = lax.axis_index("views")
    s = lax.axis_index("slab")
    slabs = lax.axis_size("slab")
    sibling = (v // 2 * 2 + 1 - lax.rem(v, 2), s)
    opposite = lax.rem(v + 2, 4)
    across = (opposite, s)
    above = (v, lax.rem(s + 1, slabs))
    below = (v, lax.rem(s + slabs - 1, slabs))

    has_above = s < slabs - 1
    has_below = s > 0

    barrier = pltpu.get_barrier_semaphore()

    def greet(device):
        pl.semaphore_signal(barrier, inc=1, device_id=device, device_id_type=MESH)

    greet(sibling)
    greet(across)
    pl.when(has_above)(lambda: greet(above))
    pl.when(has_below)(lambda: greet(below))

    class Copy:
        def __init__(self, src, dst, send, recv, device, there=None, here=None):
            self.there, self.here = there, here
            self.copy = pltpu.make_async_remote_copy(
                src_ref=src, dst_ref=dst, send_sem=send, recv_sem=recv, device_id=device, device_id_type=MESH
            )

        def on(self, condition, step):
            if condition is None:
                step()
            else:
                pl.when(condition)(step)

        def start(self):
            self.on(self.there, self.copy.start)

        def wait_send(self):
            self.on(self.there, self.copy.wait_send)

        def wait_recv(self):
            self.on(self.here, self.copy.wait_recv)

    piece_rows = piece * lors
    tile_loads = [
        pltpu.make_async_copy(
            tiles_hbm.at[pl.ds(n * piece_rows, piece_rows)], tiles.at[pl.ds(n * piece_rows, piece_rows)], tile_sem.at[n]
        )
        for n in range(PIECES)
    ]
    for load in tile_loads:
        load.start()

    def raw_load(m, slot):
        lanes = 2 * QUAD * LANES
        start = m * lanes if isinstance(m, int) else pl.multiple_of(m * lanes, lanes)
        return pltpu.make_async_copy(kw_hbm.at[:, pl.ds(start, lanes)], raw.at[slot], raw_sem.at[slot])

    for m in range(RING):
        raw_load(m, m).start()

    def sides(for_above, for_below):
        return ((for_above, above, has_above, has_below), (for_below, below, has_below, has_above))

    def begin(pair):
        for copy in pair:
            copy.start()

    to_x, to_fwd, key_copies = [], [], []
    for n in range(PIECES):
        rows = pl.ds(n * piece, piece)
        pair = []
        for side, (target, device, there, here) in enumerate(sides(1, 2)):
            pair.append(
                Copy(
                    contrib.at[0, rows], contrib.at[target, rows], raw_send.at[side, n], raw_recv.at[side, n],
                    device, there, here,
                )
            )
        to_x.append(pair)
        to_fwd.append(
            [
                Copy(
                    contrib.at[side + 1, rows], contrib.at[side + 4, rows],
                    fwd_send.at[side, n], fwd_recv.at[side, n], sibling, has, has,
                )
                for side, has in enumerate((has_below, has_above))
            ]
        )
    for n, (source, target, device, there, here) in enumerate(
        (
            (0, 1, above, has_above, has_below),
            (0, 2, below, has_below, has_above),
            (0, 3, sibling, None, None),
            (1, 4, sibling, has_below, has_below),
            (2, 5, sibling, has_above, has_above),
        )
    ):
        key_copies.append(
            Copy(keys.at[source], keys.at[target], key_send.at[n], key_recv.at[n], device, there, here)
        )
    to_sibling = Copy(contrib.at[0], contrib.at[3], sib_send.at[0], sib_recv.at[0], sibling)

    def nothing(plane_at, sets):
        plane[plane_at] = jnp.zeros(plane.shape[1:], jnp.float32)
        for index in sets:
            contrib[index] = jnp.zeros(contrib.shape[1:], jnp.float32)
            keys[index] = jnp.full(keys.shape[1:], -1, jnp.int32)

    pl.when(jnp.logical_not(has_below))(lambda: nothing(0, (1, 4)))
    pl.when(jnp.logical_not(has_above))(lambda: nothing(2, (2, 5)))

    width = keys.shape[2]
    pad = jnp.full((1, width - count), -1, jnp.int32)
    row = jnp.concatenate([map_ref[u] for u in range(subsets)] + [pad], axis=1)
    keys[0] = jnp.broadcast_to(row, keys.shape[1:])
    spread = (
        lax.rem(lax.broadcasted_iota(jnp.int32, (lors, BLOCK), 1), lors)
        == lax.broadcasted_iota(jnp.int32, (lors, BLOCK), 0)
    ).astype(jnp.float32).astype(jnp.bfloat16)
    group = BLOCK // lors
    diagonal = (
        lax.rem(lax.broadcasted_iota(jnp.int32, (per_dev, BLOCK), 0), group)
        == lax.broadcasted_iota(jnp.int32, (per_dev, BLOCK), 1) // lors
    )
    wide = []
    for u in range(subsets):
        spread_out = lax.dot_general(
            lor_ref[u], spread, (((0,), (0,)), ((), ())), preferred_element_type=jnp.float32
        )
        wide.append(jnp.where(diagonal, spread_out, 0.0).astype(jnp.bfloat16))
    for n in range(PIECES):
        tile_loads[n].wait()
        for first in range(n * piece, (n + 1) * piece, group):
            own = first % per_dev
            contrib[0, pl.ds(first, group), :] = jnp.dot(
                wide[first // per_dev][own : own + group], tiles[pl.ds(first * lors, BLOCK), :],
                preferred_element_type=jnp.float32,
            )
        if n == 0:
            pl.semaphore_wait(barrier, 2 + has_above.astype(jnp.int32) + has_below.astype(jnp.int32))
            for k in range(3):
                key_copies[k].start()
        begin(to_x[n])
    lane16 = lax.broadcasted_iota(jnp.int32, (16, LANES), 1)

    def turn(slot, m):
        for base in range(0, entries, 16):
            size = min(16, entries - base)
            for quad in range(2):
                here = [raw[slot, pl.ds(base, size), pl.ds((quad * QUAD + c) * LANES, LANES)] for c in range(QUAD)]
                for i in range(4):
                    first, a = divmod(NCOL * i, LANES)
                    for q in range(PARTS):
                        values = here[first + q]
                        if a:
                            if first + q + 1 < QUAD:
                                values = jnp.where(lane16[0:size] >= a, values, here[first + q + 1])
                            values = pltpu.roll(values, LANES - a, 1)
                        values = values.astype(jnp.float32)
                        for half in range(0, size, 8):
                            some = min(8, size - half)
                            stage[(base + half) // 8 * PARTS + q, pl.ds((4 * quad + i) * 8, some), :] = values[
                                half : half + some
                            ]
            for e in range(base, base + size, 2):
                for q in range(PARTS):
                    block = e // 8 * PARTS + q
                    both = [stage[block, pl.ds(min(e + n, entries - 1) % 8, 8, stride=8), :] for n in range(2)]
                    weights[block, pl.ds(pl.multiple_of(m * 64 + e % 8 * 8, 16), 16), :] = jnp.concatenate(
                        both, axis=0
                    ).astype(jnp.bfloat16)

    def turn_pairs(low, high):
        @pl.loop(low, high)
        def _(m):
            slot = lax.rem(m, RING)
            raw_load(m, slot).wait()
            turn(slot, m)

            @pl.when(m + RING < pairs)
            def _():
                raw_load(m + RING, slot).start()

    def scatter(sets, into, first, start, stop):
        for index in sets:
            delta = (0, -1, 1)[index % 3]
            whole = contrib[index, start:stop, :]
            high = whole.astype(jnp.bfloat16)
            low = (whole - high.astype(jnp.float32)).astype(jnp.bfloat16)
            place = keys[index][0:1, start:stop] - plane_blocks * (1 - delta)
            inside = (place >= 0) & (place < plane_blocks)
            for n, view in enumerate((opposite, v)):
                target = jnp.where(inside, place - (band_blocks * view - HALO), -1)
                chosen = lax.broadcasted_iota(jnp.int32, (BANDED, stop - start), 0) == target
                chosen = jnp.where(chosen, 1.0, 0.0).astype(jnp.bfloat16)
                total = jnp.dot(chosen, high, preferred_element_type=jnp.float32) + jnp.dot(
                    chosen, low, preferred_element_type=jnp.float32
                )
                if first and index == sets[0]:
                    into[n] = total
                else:
                    into[n] = into[n] + total

    to_sibling.start()
    turn_pairs(0, pairs)
    for k in range(2):
        key_copies[k].wait_recv()
        key_copies[3 + k].start()
    for n in range(AHEAD):
        for side in range(2):
            to_x[n][side].wait_recv()
            to_fwd[n][side].start()
    for n in range(AHEAD, PIECES):
        for side in range(2):
            to_x[n][side].wait_recv()
            to_fwd[n][side].start()
    key_copies[2].wait_recv()
    to_sibling.wait_recv()
    scatter((0, 3, 1, 2), band, True, 0, count)
    for k in range(2):
        key_copies[3 + k].wait_recv()
    for n in range(PIECES):
        for side in range(2):
            to_fwd[n][side].wait_recv()
        if n == PIECES - 2:
            scatter((4, 5), band, False, 0, count - piece)
    scatter((4, 5), band, False, count - piece, count)

    for half in range(2):
        lanes = pl.ds(half * LANES, LANES)
        zsend[pl.ds(half, BANDED, stride=2), :] = band[0, :, lanes]
    chunk_rows = [pl.ds(MARKS[c], MARKS[c + 1] - MARKS[c]) for c in range(CHUNKS)]
    to_across = [
        Copy(zsend.at[rows], zrecv.at[rows], z_send.at[c], z_recv.at[c], across) for c, rows in enumerate(chunk_rows)
    ]
    for c in range(AHEAD):
        to_across[c].start()
    for half in range(2):
        lanes = pl.ds(half * LANES, LANES)
        plane[1, pl.ds(half, BANDED, stride=2), :] = band[1, :, lanes]
    for c in range(AHEAD, CHUNKS):
        to_across[c - AHEAD].wait_send()
        to_across[c].start()

    lane = lax.broadcasted_iota(jnp.int32, (8, LANES), 1)

    def shift(d, part):
        rows = {}

        def at(c):
            if c not in rows:
                rows[c] = plane[d, pl.ds(8 * QUAD * part + c, 8, stride=QUAD), :]
            return rows[c]

        for i in range(4):
            for q in range(PARTS):
                for dx in range(-3, 4):
                    c, a = divmod(LEAD + NCOL * i + LANES * q + dx, LANES)
                    moved = at(c)
                    if a:
                        moved = pltpu.roll(jnp.where(lane >= a, moved, at(c + 1)), LANES - a, 1)
                    if q == 0 and dx < 0:
                        moved = jnp.where(lane >= -dx, moved, 0.0)
                    if q == PARTS - 1 and dx > 0:
                        moved = jnp.where(lane < NCOL - LANES * q - dx, moved, 0.0)
                    shifted[(d * 7 + dx + 3) * PARTS + q, pl.ds(32 * part + i, 8, stride=4), :] = moved

    def box(planes, t, q):
        sums = [None] * 2
        for pair in range(0, entries, 2):
            wanted = [e for e in (pair, pair + 1) if e < entries and e // 49 in planes]
            if not wanted:
                continue
            both = weights[
                pair // 8 * PARTS + q, pl.ds(pl.multiple_of(t * 64 + pair % 8 * 8, 16), 16), :
            ].astype(jnp.float32)
            for e in wanted:
                d, dy, dx = e // 49, e // 7 % 7, e % 7
                n = e % 2
                term = both[8 * n : 8 * n + 8] * shifted[(d * 7 + dx) * PARTS + q, pl.ds(t * 8 + dy, 8), :]
                sums[n] = term if sums[n] is None else sums[n] + term
        return sums[0] + sums[1]

    def box_rows(planes, low, high, first):
        @pl.loop(low, high)
        def _(t):
            rows = pl.ds(pl.multiple_of(t * 8, 8), 8)
            for q in range(PARTS):
                total = box(planes, t, q)
                result[q, rows, :] = total if first else result[q, rows, :] + total

    def flatten(part):
        some = min(8, quads - 8 * part)
        pieces = [[] for _ in range(QUAD + 1)]
        for i in range(4):
            for q in range(PARTS):
                values = result[q, pl.ds(32 * part + i, some, stride=4), :]
                c, a = divmod(NCOL * i + LANES * q, LANES)
                end = a + min(LANES, NCOL - LANES * q)
                if a:
                    values = pltpu.roll(values, a, 1)
                pieces[c].append((a, values))
                if end > LANES:
                    pieces[c + 1].append((0, values))
        for c in range(QUAD):
            total = None
            for low, values in sorted(pieces[c], key=lambda piece: piece[0]):
                total = values if total is None else jnp.where(lane[0:some] >= low, values, total)
            out_ref[pl.ds(8 * QUAD * part + c, some, stride=QUAD), 0, :] = total

    to_sides = []
    for c in range(CHUNKS):
        rows = chunk_rows[c]
        to_across[c].wait_recv()
        plane[1, rows, :] = plane[1, rows, :] + zrecv[rows, :]
        to_sides.append(
            [
                Copy(
                    plane.at[1, rows], plane.at[target, rows], x_send.at[side, c], x_recv.at[side, c],
                    device, there, here,
                )
                for side, (target, device, there, here) in enumerate(sides(0, 2))
            ]
        )
        begin(to_sides[c])
        shift(1, c)
        box_rows((1,), BOX_MARKS[c], BOX_MARKS[c + 1], True)
    for c in range(CHUNKS):
        for copy in to_sides[c]:
            copy.wait_recv()
        shift(0, c)
        shift(2, c)
        box_rows((0, 2), BOX_MARKS[c], BOX_MARKS[c + 1], False)
        if c:
            flatten(c - 1)
    flatten(CHUNKS - 1)

    for copies in to_x + to_fwd + to_sides + [to_across[CHUNKS - AHEAD :], key_copies, [to_sibling]]:
        for copy in copies:
            copy.wait_send()


def per_device(tiles, lor_weight, block_map, kernel_weight):
    subsets, _, per_dev, lors, width = tiles.shape
    entries, planes, voxels = kernel_weight.shape
    plane_blocks = voxels * lax.axis_size("views") // width
    count = subsets * per_dev
    out_rows = voxels // LANES
    image_rows = voxels // NCOL
    groups = -(-entries // 8)
    hbm = pl.BlockSpec(memory_space=pl.ANY)
    vmem = pl.BlockSpec(memory_space=pltpu.VMEM)
    dma = pltpu.SemaphoreType.DMA
    out = pl.pallas_call(
        functools.partial(kernel, plane_blocks),
        out_shape=jax.ShapeDtypeStruct((out_rows, 1, LANES), jnp.float32),
        in_specs=[hbm, vmem, vmem, hbm],
        out_specs=vmem,
        scratch_shapes=[
            pltpu.VMEM((count * lors, width), jnp.bfloat16),
            pltpu.VMEM((RING, entries, 2 * QUAD * LANES), jnp.bfloat16),
            pltpu.VMEM((groups * PARTS, 64, LANES), jnp.float32),
            pltpu.VMEM((groups * PARTS, image_rows * 8, LANES), jnp.bfloat16),
            pltpu.VMEM((6, count, width), jnp.float32),
            pltpu.VMEM((6, 8, 384), jnp.int32),
            pltpu.VMEM((2, BANDED, width), jnp.float32),
            pltpu.VMEM((ROWS, LANES), jnp.float32),
            pltpu.VMEM((ROWS, LANES), jnp.float32),
            pltpu.VMEM((3, ROWS + 8, LANES), jnp.float32),
            pltpu.VMEM((21 * PARTS, 128, LANES), jnp.float32),
            pltpu.VMEM((PARTS, 128, LANES), jnp.float32),
            dma((PIECES,)),
            dma((RING,)),
            dma((2, PIECES)),
            dma((2, PIECES)),
            dma((1,)),
            dma((1,)),
            dma((2, PIECES)),
            dma((2, PIECES)),
            dma((5,)),
            dma((5,)),
            dma((CHUNKS,)),
            dma((CHUNKS,)),
            dma((2, CHUNKS)),
            dma((2, CHUNKS)),
        ],
        compiler_params=pltpu.CompilerParams(
            collective_id=0, has_side_effects=True, vmem_limit_bytes=60 * 1024 * 1024
        ),
    )(
        tiles.reshape(count * lors, width),
        jnp.transpose(lor_weight.reshape(subsets, per_dev, lors), (0, 2, 1)),
        block_map.reshape(subsets, 1, per_dev),
        kernel_weight.reshape(entries, voxels),
    )
    return out.reshape(planes, voxels)


def solution(mesh):
    placed = (
        P(None, "slab", "views", None, None),
        P(None, "slab", "views", None),
        P(None, "slab", "views"),
        P(None, "slab", "views"),
    )
    return jax.shard_map(
        per_device, mesh=mesh, in_specs=placed, out_specs=P("slab", "views"), check_vma=False
    )
```
